512 devices in a mesh: inp: 128 (over y, z_hi, x, core), tm: 4 (over z_lo).
Axes of the slice: x: 4, y: 8, z: 8 (z_hi: 2, z_lo: 4; z = z_hi * 4 + z_lo), core: 2. Of those that a mesh axis runs over, the one named last changes fastest.
Arguments:
- raw_samples: bfloat16 [1024, 262144], P('inp', 'tm'), may hold values from -6 to 6
- filter_taps: float32 [4, 2048], replicated, may hold values from -3 to 3
Outputs:
- visibilities: float32 [128, 1024, 1024], P('inp', 'tm')
The draws below stay inside these ranges and needn't reach their ends.
All inputs are finite; a program needn't handle non-finite values.
Results may differ from the reference program's by a relative error of at most 0.014.
Values may be sent and summed in bfloat16 or wider, within the bound.
A program may use at most 64 MiB of HBM per device.

```python
import math
import jax
import jax.numpy as jnp
from jax import lax

INPUTS = 1024
NFFT = 2048
TAPS = 4
FR_DEV = 32
FRAMES = 128
CH = 128


def draw_raw_samples(key, part):
    key = jax.random.fold_in(key, 11)
    frame_index = jnp.arange(FRAMES, dtype=jnp.int32)
    block_edge = frame_index % FR_DEV >= FR_DEV - (TAPS - 1)
    drawn = jax.random.normal(key, (INPUTS, FRAMES, NFFT), jnp.float32)
    scales = jnp.where(block_edge, 3.0, 0.4).astype(jnp.float32)
    values = jnp.clip(drawn * scales[None, :, None], -6.0, 6.0)
    return values.reshape(INPUTS, FRAMES * NFFT).astype(jnp.bfloat16)


def noise(own_key, extent, scale, most, held_as=jnp.bfloat16):
    return jnp.clip(scale * jax.random.normal(own_key, extent, jnp.float32), -most, most).astype(held_as)


def setup_inputs(seed: int = 0) -> dict:
    splits = jax.random.split(jax.random.key(seed), 3)
    raw_samples = draw_raw_samples(jax.random.fold_in(splits[2], 71), 0)
    filter_taps = noise(splits[1], (TAPS, NFFT), 1.0, 3.0, jnp.float32)
    return {"raw_samples": raw_samples, "filter_taps": filter_taps}


def fourier_table(length, channels):
    sample_index = jnp.arange(length, dtype=jnp.int32)[:, None]
    channel_index = jnp.arange(1, channels + 1, dtype=jnp.int32)[None, :]
    angles = (sample_index * channel_index % length).astype(jnp.float32) * (2.0 * math.pi / length)
    return jnp.concatenate([jnp.cos(angles), -jnp.sin(angles)], axis=1).astype(jnp.bfloat16)

def polyphase(frames, filter_taps, earlier):
    taps = filter_taps.shape[0]
    frame_count = frames.shape[1]
    padded = jnp.concatenate([earlier, frames], axis=1).astype(jnp.float32)
    running = jnp.zeros(frames.shape, jnp.float32)
    for tap_index in range(taps):
        begin = taps - 1 - tap_index
        running = running + filter_taps[tap_index] * padded[:, begin:begin + frame_count, :]
    return running.astype(jnp.bfloat16)

def pack_triangle(real_part, imag_part, row_offset, col_offset):
    row_index = row_offset + jnp.arange(real_part.shape[0], dtype=jnp.int32)[:, None]
    col_index = col_offset + jnp.arange(real_part.shape[1], dtype=jnp.int32)[None, :]
    return jnp.where(row_index <= col_index, real_part, imag_part)

def contract(left, right):
    return lax.dot_general(left, right, (((1,), (1,)), ((), ())), preferred_element_type=jnp.float32)

def reference(raw_samples, filter_taps):
    taps = filter_taps.shape[0]
    group_size = math.gcd(INPUTS, 64)
    table = fourier_table(NFFT, CH)
    frames = raw_samples.reshape(INPUTS // group_size, group_size, FRAMES, NFFT)

    def channelize(group):
        earlier = jnp.zeros((group_size, taps - 1, NFFT), jnp.bfloat16)
        filtered = polyphase(group, filter_taps, earlier)
        spectra = jnp.dot(filtered.reshape(group_size * FRAMES, NFFT), table, preferred_element_type=jnp.float32)
        spectra = (spectra * (1.0 / math.sqrt(NFFT))).astype(jnp.bfloat16)
        return spectra.reshape(group_size, FRAMES, 2 * CH)
    spectra = lax.map(channelize, frames).reshape(INPUTS, FRAMES, 2, CH)
    per_channel = jnp.transpose(spectra, (3, 2, 0, 1))

    def correlate(channel):
        real_part, imag_part = (channel[0], channel[1])
        stacked = jnp.concatenate([real_part, imag_part], axis=1)
        rotated = jnp.concatenate([imag_part, -real_part], axis=1)
        both_rows = jnp.concatenate([stacked, rotated], axis=0)
        product = contract(both_rows, stacked)
        packed = pack_triangle(product[:INPUTS], product[INPUTS:], 0, 0)
        return packed * jnp.float32(1.0 / FRAMES)
    return lax.map(correlate, per_channel)
```

```python
import math

import jax
import jax.numpy as jnp
import numpy as np
from jax import lax
from jax.experimental import pallas as pl
from jax.experimental.pallas import tpu as pltpu
from jax.sharding import PartitionSpec as P

MESH = pl.DeviceIdType.MESH
NFFT = 2048
TAPS = 4
FRAMES = 32
ALL_FRAMES = 128
PLANE = 64
LANES = 128
CHUNK = 512
SCALE = 1.0 / math.sqrt(NFFT)


def table_rows():
    row = np.arange(4 * PLANE)
    part, z_hi, dest = row % 2, row // 2 % 2, row // 4
    channel = ((dest // 8) * 2 + z_hi) * 8 + dest % 8
    n = np.arange(NFFT)
    m = (n[None, :] * (channel[:, None] + 1)) % NFFT
    angles = m.astype(np.float32) * np.float32(2.0 * math.pi / NFFT)
    rows = np.where(part[:, None] == 0, np.cos(angles), -np.sin(angles))
    return rows.astype(np.float32).astype(jnp.bfloat16)


def nt(left, right):
    return lax.dot_general(
        left, right, (((1,), (1,)), ((), ())), preferred_element_type=jnp.float32
    )


def nn(left, right):
    return lax.dot_general(
        left, right, (((1,), (0,)), ((), ())), preferred_element_type=jnp.float32
    )


def filter_frames(first, last, taps_v, raw_v, halo_v, filt_v):
    def step(c, carry):
        base = pl.multiple_of(c * CHUNK, CHUNK)
        taps = [taps_v[k : k + 1, pl.ds(base, CHUNK)] for k in range(TAPS)]

        def frame(f):
            if f < 0:
                ref, at = halo_v, (f + TAPS - 1) * NFFT
            else:
                ref, at = raw_v, f * NFFT
            at = pl.multiple_of(base + at, CHUNK)
            return ref[:, pl.ds(at, CHUNK)].astype(jnp.float32)

        window = [frame(first - k) for k in range(TAPS)]
        done = []
        for f in range(first, last):
            if f > first:
                window = [frame(f)] + window[: TAPS - 1]
            total = taps[0] * window[0]
            for k in range(1, TAPS):
                total = total + taps[k] * window[k]
            done.append(total)
            if len(done) == 2:
                pair = jnp.concatenate(done, axis=0).astype(jnp.bfloat16)
                filt_v[(f - 1) * 8 : (f + 1) * 8, pl.ds(base, CHUNK)] = pair
                done = []
        return carry

    lax.fori_loop(0, NFFT // CHUNK, step, 0)


def turn(rows):
    lane = lax.broadcasted_iota(jnp.int32, (8, LANES), 1)
    for b in range(4):
        step, width = 1 << b, 8 << b
        low = (lane & width) == 0
        out = list(rows)
        for s in range(16):
            if s & step == 0:
                x, y = rows[s], rows[s + step]
                out[s] = jnp.where(low, x, pltpu.roll(y, width, 1))
                out[s + step] = jnp.where(low, pltpu.roll(x, LANES - width, 1), y)
        rows = out
    return rows


def kernel(
    raw, taps, table, out,
    raw_v, taps_v, table_v, halo_v, filt_v, sbuf, rbuf, xs, xr, lt,
    in_sem, halo_ssem, halo_rsem, ssem, rsem, zssem, zrsem,
):
    me = lax.axis_index("inp")
    t = lax.axis_index("tm")
    y, zh, xc = me // 16, (me // 8) % 2, me % 8
    mine = y * 8 + xc
    my_m, my_lo = mine // 16, mine % 16
    my_z = zh * 4 + t

    def plane(d):
        return ((d // 8) * 16 + zh * 8 + d % 8, t)

    def column(z):
        return (y * 16 + (z // 4) * 8 + xc, z % 4)

    loads = [
        pltpu.make_async_copy(table, table_v, in_sem.at[0]),
        pltpu.make_async_copy(taps, taps_v, in_sem.at[1]),
        pltpu.make_async_copy(raw, raw_v, in_sem.at[2]),
    ]
    for load in loads:
        load.start()

    barrier = pltpu.get_barrier_semaphore()
    for k in range(1, 8):
        pl.semaphore_signal(
            barrier, inc=1, device_id=column((my_z + k) % 8), device_id_type=MESH
        )

    def greet(k, carry):
        pl.semaphore_signal(
            barrier, inc=1, device_id=plane((mine + k) % PLANE), device_id_type=MESH
        )
        return carry

    lax.fori_loop(1, PLANE, greet, 0)
    pl.semaphore_wait(barrier, PLANE - 1 + 7)

    halo = pltpu.make_async_remote_copy(
        src_ref=raw.at[:, pl.ds((FRAMES - TAPS + 1) * NFFT, (TAPS - 1) * NFFT)],
        dst_ref=halo_v,
        send_sem=halo_ssem,
        recv_sem=halo_rsem,
        device_id=(me, (t + 1) % 4),
        device_id_type=MESH,
    )

    @pl.when(t < 3)
    def _():
        halo.start()

    for load in loads:
        load.wait()
    filter_frames(4, FRAMES, taps_v, raw_v, halo_v, filt_v)
    s1 = nt(table_v[...], filt_v[LANES:, :])

    @pl.when(t > 0)
    def _():
        halo.wait_recv()

    @pl.when(t == 0)
    def _():
        halo_v[...] = jnp.zeros_like(halo_v)

    filter_frames(0, 4, taps_v, raw_v, halo_v, filt_v)
    s0 = nt(table_v[...], filt_v[:LANES, :])
    s0 = (s0 * SCALE).reshape(PLANE // 2, 8, LANES)
    s1 = (s1 * SCALE).reshape(PLANE // 2, 8, LANES)
    first = lax.broadcasted_iota(jnp.int32, (PLANE // 2, 8, LANES), 1) < 4
    sbuf[:, 0] = jnp.where(first, s0, pltpu.roll(s1, 4, 1)).astype(jnp.bfloat16)
    sbuf[:, 1] = jnp.where(first, pltpu.roll(s0, 4, 1), s1).astype(jnp.bfloat16)

    own = pltpu.make_async_copy(
        sbuf.at[mine // 2, mine % 2], rbuf.at[mine], rsem.at[my_m]
    )
    own.start()

    def send(k, carry):
        d = ((my_m + k // 16) % 4) * 16 + (my_lo + k % 16) % 16
        pltpu.make_async_remote_copy(
            src_ref=sbuf.at[d // 2, d % 2],
            dst_ref=rbuf.at[mine],
            send_sem=ssem,
            recv_sem=rsem.at[my_m],
            device_id=plane(d),
            device_id_type=MESH,
        ).start()
        return carry

    lax.fori_loop(1, PLANE, send, 0)

    sub = lax.broadcasted_iota(jnp.int32, (8, LANES), 0)

    def relay(j, carry):
        m = (my_m - j + 4) % 4
        got = rbuf.at[pl.ds(m * 16, 16)]
        pltpu.make_async_copy(got, got, rsem.at[m]).wait()
        rows = turn([rbuf[m * 16 + s].astype(jnp.float32) for s in range(16)])
        halves = ([], [])
        for p in range(8):
            a, b = rows[2 * p], rows[2 * p + 1]
            halves[0].append(jnp.where((sub & 2) == 0, a, pltpu.roll(b, 2, 0)))
            halves[1].append(jnp.where((sub & 2) == 0, pltpu.roll(a, 6, 0), b))
        for h in range(2):
            for q in range(4):
                pair = jnp.concatenate(halves[h][2 * q : 2 * q + 2], axis=0)
                xs[m, h, 16 * q : 16 * q + 16, :] = pair.astype(jnp.bfloat16)
        pltpu.make_async_copy(xs.at[m, zh], xr.at[m, my_z], zrsem.at[m]).start()
        for k in (4, 3, 5, 2, 6, 1, 7):
            z = (my_z + k) % 8
            pltpu.make_async_remote_copy(
                src_ref=xs.at[m, z // 4],
                dst_ref=xr.at[m, my_z],
                send_sem=zssem.at[m],
                recv_sem=zrsem.at[m],
                device_id=column(z),
                device_id_type=MESH,
            ).start()
        return carry

    lax.fori_loop(0, 4, relay, 0)

    for m in range(4):
        pltpu.make_async_copy(xr.at[m], xr.at[m], zrsem.at[m]).wait()

    def block(m):
        both = [xr[m, 4 * z : 4 * z + 4].reshape(256, LANES) for z in range(2)]
        return jnp.concatenate(both, axis=1)

    held = block(t).astype(jnp.float32)
    grouped = held.reshape(32, 8, 256)
    even = lax.broadcasted_iota(jnp.int32, (32, 8, 256), 1) % 2 == 0
    swapped = jnp.where(even, pltpu.roll(grouped, 7, 1), -pltpu.roll(grouped, 1, 1))
    lt[0] = held.T.astype(jnp.bfloat16)
    lt[1] = swapped.reshape(256, 256).T.astype(jnp.bfloat16)

    lane = lax.broadcasted_iota(jnp.int32, (256, LANES), 1)

    def put(m, packed):
        packed = packed * (1.0 / ALL_FRAMES)
        a, b = packed[:, :LANES], packed[:, LANES:]
        base = pl.multiple_of(m * 256, 256)
        tiles = (
            jnp.where(lane < 64, a, pltpu.roll(b, 64, 1)),
            jnp.where(lane < 64, pltpu.roll(a, 64, 1), b),
        )
        for part, tile in enumerate(tiles):
            for z in range(2):
                for half in range(2):
                    out[
                        half * 128 + z * 64 : half * 128 + z * 64 + 64,
                        pl.ds(base + part * LANES, LANES),
                    ] = tile[z * 128 + half * 64 : z * 128 + half * 64 + 64]

    def place(index):
        return (index // 64 % 2) * 128 + (index // 128) * 64 + index % 64

    right = block(t)
    row = place(lax.broadcasted_iota(jnp.int32, (256, 256), 0))
    col = place(lax.broadcasted_iota(jnp.int32, (256, 256), 1))
    put(t, jnp.where(row <= col, nn(lt[0], right), nn(lt[1], right)))

    def other(j, carry):
        m = (t + j) % 4
        put(m, nn(lt[(m < t).astype(jnp.int32)], block(m)))
        return carry

    lax.fori_loop(1, 4, other, 0)

    @pl.when(t < 3)
    def _():
        halo.wait_send()

    sent = rbuf.at[pl.ds(0, PLANE - 1)]
    pltpu.make_async_copy(sent, sent, ssem).wait()
    for m in range(4):
        sent = xr.at[m, pl.ds(0, 7)]
        pltpu.make_async_copy(sent, sent, zssem.at[m]).wait()


def body(raw_samples, filter_taps):
    anywhere = pl.BlockSpec(memory_space=pl.ANY)
    visibilities = pl.pallas_call(
        kernel,
        out_shape=jax.ShapeDtypeStruct((256, 1024), jnp.float32),
        in_specs=[anywhere] * 3,
        out_specs=pl.BlockSpec(memory_space=pltpu.VMEM),
        scratch_shapes=[
            pltpu.VMEM((8, FRAMES * NFFT), jnp.bfloat16),
            pltpu.VMEM((TAPS, NFFT), jnp.float32),
            pltpu.VMEM((4 * PLANE, NFFT), jnp.bfloat16),
            pltpu.VMEM((8, (TAPS - 1) * NFFT), jnp.bfloat16),
            pltpu.VMEM((8 * FRAMES, NFFT), jnp.bfloat16),
            pltpu.VMEM((PLANE // 2, 2, 8, LANES), jnp.bfloat16),
            pltpu.VMEM((PLANE, 8, LANES), jnp.bfloat16),
            pltpu.VMEM((4, 2, 64, LANES), jnp.bfloat16),
            pltpu.VMEM((4, 8, 64, LANES), jnp.bfloat16),
            pltpu.VMEM((2, 256, 256), jnp.bfloat16),
            pltpu.SemaphoreType.DMA((3,)),
            pltpu.SemaphoreType.DMA,
            pltpu.SemaphoreType.DMA,
            pltpu.SemaphoreType.DMA,
            pltpu.SemaphoreType.DMA((4,)),
            pltpu.SemaphoreType.DMA((4,)),
            pltpu.SemaphoreType.DMA((4,)),
        ],
        compiler_params=pltpu.CompilerParams(
            collective_id=0, has_side_effects=True, vmem_limit_bytes=40 << 20
        ),
    )(raw_samples, filter_taps, jnp.asarray(table_rows()))
    return visibilities[None]


def solution(mesh):
    return jax.shard_map(
        body,
        mesh=mesh,
        in_specs=(P("inp", "tm"), P()),
        out_specs=P("inp", "tm", None),
        check_vma=False,
    )
```

```python
import math

import jax
import jax.numpy as jnp
import numpy as np
from jax import lax
from jax.experimental import pallas as pl
from jax.experimental.pallas import tpu as pltpu
from jax.sharding import PartitionSpec as P

MESH = pl.DeviceIdType.MESH
NFFT = 2048
TAPS = 4
FRAMES = 32
ALL_FRAMES = 128
PLANE = 64
LANES = 128
TAIL = 8 * (TAPS - 1)
CHUNK = 512
SCALE = 1.0 / math.sqrt(NFFT)


def table_rows():
    row = np.arange(4 * PLANE)
    part, z_hi, dest = row % 2, row // 2 % 2, row // 4
    channel = ((dest // 8) * 2 + z_hi) * 8 + dest % 8
    n = np.arange(NFFT)
    m = (n[None, :] * (channel[:, None] + 1)) % NFFT
    angles = m.astype(np.float32) * np.float32(2.0 * math.pi / NFFT)
    rows = np.where(part[:, None] == 0, np.cos(angles), -np.sin(angles))
    return rows.astype(np.float32).astype(jnp.bfloat16)


def nt(left, right):
    return lax.dot_general(
        left, right, (((1,), (1,)), ((), ())), preferred_element_type=jnp.float32
    )


def nn(left, right):
    return lax.dot_general(
        left, right, (((1,), (0,)), ((), ())), preferred_element_type=jnp.float32
    )


def filter_frames(first, last, taps_v, raw_v, filt_v):
    def step(c, carry):
        base = pl.multiple_of(c * CHUNK, CHUNK)
        taps = [taps_v[k : k + 1, pl.ds(base, CHUNK)] for k in range(TAPS)]

        def frame(f):
            if not 0 <= f < FRAMES:
                return None
            at = pl.multiple_of(base + f * NFFT, CHUNK)
            return raw_v[:, pl.ds(at, CHUNK)].astype(jnp.float32)

        window = [frame(first - k) for k in range(TAPS)]
        done = []
        for f in range(first, last):
            if f > first:
                window = [frame(f)] + window[: TAPS - 1]
            total = jnp.zeros((8, CHUNK), jnp.float32)
            for k in range(TAPS):
                if window[k] is not None:
                    total = total + taps[k] * window[k]
            done.append(total)
            if len(done) == 2:
                pair = jnp.concatenate(done, axis=0).astype(jnp.bfloat16)
                filt_v[(f - 1) * 8 : (f + 1) * 8, pl.ds(base, CHUNK)] = pair
                done = []
        return carry

    lax.fori_loop(0, NFFT // CHUNK, step, 0)


def turn(rows):
    lane = lax.broadcasted_iota(jnp.int32, (8, LANES), 1)
    for b in range(4):
        step, width = 1 << b, 8 << b
        low = (lane & width) == 0
        out = list(rows)
        for s in range(16):
            if s & step == 0:
                x, y = rows[s], rows[s + step]
                out[s] = jnp.where(low, x, pltpu.roll(y, width, 1))
                out[s + step] = jnp.where(low, pltpu.roll(x, LANES - width, 1), y)
        rows = out
    return rows


def kernel(
    raw, taps, table, out,
    raw_v, taps_v, table_v, filt_v, tail_s, tail_r, sbuf, rbuf, xs, xr, lt,
    in_sem, tail_ssem, tail_rsem, ssem, rsem, zssem, zrsem, fssem, frsem,
):
    me = lax.axis_index("inp")
    t = lax.axis_index("tm")
    y, zh, xc = me // 16, (me // 8) % 2, me % 8
    mine = y * 8 + xc
    my_m, my_lo = mine // 16, mine % 16
    my_z = zh * 4 + t

    def plane(d):
        return ((d // 8) * 16 + zh * 8 + d % 8, t)

    def column(half, at):
        return (y * 16 + half * 8 + xc, at)

    loads = [
        pltpu.make_async_copy(table, table_v, in_sem.at[0]),
        pltpu.make_async_copy(taps, taps_v, in_sem.at[1]),
        pltpu.make_async_copy(raw, raw_v, in_sem.at[2]),
    ]
    for load in loads:
        load.start()

    barrier = pltpu.get_barrier_semaphore()
    for k in range(1, 8):
        pl.semaphore_signal(
            barrier, inc=1, device_id=column((my_z + k) % 8 // 4, (my_z + k) % 4), device_id_type=MESH
        )

    def greet(k, carry):
        pl.semaphore_signal(
            barrier, inc=1, device_id=plane((mine + k) % PLANE), device_id_type=MESH
        )
        return carry

    lax.fori_loop(1, PLANE, greet, 0)
    for load in loads:
        load.wait()
    filter_frames(FRAMES, FRAMES + 4, taps_v, raw_v, filt_v)
    tail_s[...] = nt(filt_v[8 * FRAMES :, :], table_v[...])[:TAIL]
    filter_frames(0, FRAMES, taps_v, raw_v, filt_v)
    s0 = nt(table_v[...], filt_v[:LANES, :])
    s1 = nt(table_v[...], filt_v[LANES : 2 * LANES, :])

    pl.semaphore_wait(barrier, PLANE - 1 + 7)
    tail = pltpu.make_async_remote_copy(
        src_ref=tail_s,
        dst_ref=tail_r,
        send_sem=tail_ssem,
        recv_sem=tail_rsem,
        device_id=(me, (t + 1) % 4),
        device_id_type=MESH,
    )

    @pl.when(t < 3)
    def _():
        tail.start()

    @pl.when(t > 0)
    def _():
        tail.wait_recv()

    @pl.when(t == 0)
    def _():
        tail_r[...] = jnp.zeros_like(tail_r)

    rest = jnp.zeros((LANES - TAIL, 4 * PLANE), jnp.float32)
    s0 = s0 + jnp.concatenate([tail_r[...], rest], axis=0).T
    s0 = (s0 * SCALE).reshape(PLANE // 2, 8, LANES)
    s1 = (s1 * SCALE).reshape(PLANE // 2, 8, LANES)
    first = lax.broadcasted_iota(jnp.int32, (PLANE // 2, 8, LANES), 1) < 4
    sbuf[:, 0] = jnp.where(first, s0, pltpu.roll(s1, 4, 1)).astype(jnp.bfloat16)
    sbuf[:, 1] = jnp.where(first, pltpu.roll(s0, 4, 1), s1).astype(jnp.bfloat16)

    own = pltpu.make_async_copy(
        sbuf.at[mine // 2, mine % 2], rbuf.at[mine], rsem.at[my_m]
    )
    own.start()

    def send(k, carry):
        d = ((my_m + k // 16) % 4) * 16 + (my_lo + k % 16) % 16
        pltpu.make_async_remote_copy(
            src_ref=sbuf.at[d // 2, d % 2],
            dst_ref=rbuf.at[mine],
            send_sem=ssem,
            recv_sem=rsem.at[my_m],
            device_id=plane(d),
            device_id_type=MESH,
        ).start()
        return carry

    lax.fori_loop(1, PLANE, send, 0)

    sub = lax.broadcasted_iota(jnp.int32, (8, LANES), 0)

    def relay(j, carry):
        m = (my_m - j + 4) % 4
        got = rbuf.at[pl.ds(m * 16, 16)]
        pltpu.make_async_copy(got, got, rsem.at[m]).wait()
        rows = turn([rbuf[m * 16 + s].astype(jnp.float32) for s in range(16)])
        halves = ([], [])
        for p in range(8):
            a, b = rows[2 * p], rows[2 * p + 1]
            halves[0].append(jnp.where((sub & 2) == 0, a, pltpu.roll(b, 2, 0)))
            halves[1].append(jnp.where((sub & 2) == 0, pltpu.roll(a, 6, 0), b))
        for h in range(2):
            for q in range(4):
                pair = jnp.concatenate(halves[h][2 * q : 2 * q + 2], axis=0)
                xs[m, h, 16 * q : 16 * q + 16, :] = pair.astype(jnp.bfloat16)
        for end in (0, 3):
            pltpu.make_async_remote_copy(
                src_ref=xs.at[m, 1 - zh],
                dst_ref=xr.at[m, my_z],
                send_sem=zssem.at[m],
                recv_sem=frsem.at[m],
                device_id=column(1 - zh, end),
                device_id_type=MESH,
            ).start()
        pltpu.make_async_copy(xs.at[m, zh], xr.at[m, my_z], zrsem.at[m]).start()
        for k in (2, 1, 3):
            pltpu.make_async_remote_copy(
                src_ref=xs.at[m, zh],
                dst_ref=xr.at[m, my_z],
                send_sem=zssem.at[m],
                recv_sem=zrsem.at[m],
                device_id=column(zh, (t + k) % 4),
                device_id_type=MESH,
            ).start()
        return carry

    lax.fori_loop(0, 4, relay, 0)

    is_end = jnp.logical_or(t == 0, t == 3)
    theirs = pl.ds((1 - zh) * 4, 4)

    def forward(m):
        return pltpu.make_async_remote_copy(
            src_ref=xr.at[m, theirs],
            dst_ref=xr.at[m, theirs],
            send_sem=fssem.at[m],
            recv_sem=frsem.at[m],
            device_id=column(zh, 1 + t // 3),
            device_id_type=MESH,
        )

    def pass_on(j, carry):
        m = (my_m - j + 4) % 4
        pltpu.make_async_copy(xr.at[m, theirs], xr.at[m, theirs], frsem.at[m]).wait()

        @pl.when(is_end)
        def _():
            forward(m).start()

        return carry

    lax.fori_loop(0, 4, pass_on, 0)

    for m in range(4):
        half = xr.at[m, pl.ds(zh * 4, 4)]
        pltpu.make_async_copy(half, half, zrsem.at[m]).wait()

    def block(m):
        both = [xr[m, 4 * z : 4 * z + 4].reshape(256, LANES) for z in range(2)]
        return jnp.concatenate(both, axis=1)

    held = block(t).astype(jnp.float32)
    grouped = held.reshape(32, 8, 256)
    even = lax.broadcasted_iota(jnp.int32, (32, 8, 256), 1) % 2 == 0
    swapped = jnp.where(even, pltpu.roll(grouped, 7, 1), -pltpu.roll(grouped, 1, 1))
    lt[0] = held.T.astype(jnp.bfloat16)
    lt[1] = swapped.reshape(256, 256).T.astype(jnp.bfloat16)

    lane = lax.broadcasted_iota(jnp.int32, (256, LANES), 1)

    def put(m, packed):
        packed = packed * (1.0 / ALL_FRAMES)
        a, b = packed[:, :LANES], packed[:, LANES:]
        base = pl.multiple_of(m * 256, 256)
        tiles = (
            jnp.where(lane < 64, a, pltpu.roll(b, 64, 1)),
            jnp.where(lane < 64, pltpu.roll(a, 64, 1), b),
        )
        for part, tile in enumerate(tiles):
            for z in range(2):
                for half in range(2):
                    out[
                        half * 128 + z * 64 : half * 128 + z * 64 + 64,
                        pl.ds(base + part * LANES, LANES),
                    ] = tile[z * 128 + half * 64 : z * 128 + half * 64 + 64]

    def place(index):
        return (index // 64 % 2) * 128 + (index // 128) * 64 + index % 64

    right = block(t)
    row = place(lax.broadcasted_iota(jnp.int32, (256, 256), 0))
    col = place(lax.broadcasted_iota(jnp.int32, (256, 256), 1))
    put(t, jnp.where(row <= col, nn(lt[0], right), nn(lt[1], right)))

    def other(j, carry):
        m = (t + j) % 4
        put(m, nn(lt[(m < t).astype(jnp.int32)], block(m)))
        return carry

    lax.fori_loop(1, 4, other, 0)

    @pl.when(t < 3)
    def _():
        tail.wait_send()

    sent = rbuf.at[pl.ds(0, PLANE - 1)]
    pltpu.make_async_copy(sent, sent, ssem).wait()
    for m in range(4):
        sent = xr.at[m, pl.ds(0, 5)]
        pltpu.make_async_copy(sent, sent, zssem.at[m]).wait()

    @pl.when(is_end)
    def _():
        for m in range(4):
            forward(m).wait_send()


def body(raw_samples, filter_taps):
    anywhere = pl.BlockSpec(memory_space=pl.ANY)
    visibilities = pl.pallas_call(
        kernel,
        out_shape=jax.ShapeDtypeStruct((256, 1024), jnp.float32),
        in_specs=[anywhere] * 3,
        out_specs=pl.BlockSpec(memory_space=pltpu.VMEM),
        scratch_shapes=[
            pltpu.VMEM((8, FRAMES * NFFT), jnp.bfloat16),
            pltpu.VMEM((TAPS, NFFT), jnp.float32),
            pltpu.VMEM((4 * PLANE, NFFT), jnp.bfloat16),
            pltpu.VMEM((8 * FRAMES + 32, NFFT), jnp.bfloat16),
            pltpu.VMEM((TAIL, 4 * PLANE), jnp.float32),
            pltpu.VMEM((TAIL, 4 * PLANE), jnp.float32),
            pltpu.VMEM((PLANE // 2, 2, 8, LANES), jnp.bfloat16),
            pltpu.VMEM((PLANE, 8, LANES), jnp.bfloat16),
            pltpu.VMEM((4, 2, 64, LANES), jnp.bfloat16),
            pltpu.VMEM((4, 8, 64, LANES), jnp.bfloat16),
            pltpu.VMEM((2, 256, 256), jnp.bfloat16),
            pltpu.SemaphoreType.DMA((3,)),
            pltpu.SemaphoreType.DMA,
            pltpu.SemaphoreType.DMA,
            pltpu.SemaphoreType.DMA,
            pltpu.SemaphoreType.DMA((4,)),
            pltpu.SemaphoreType.DMA((4,)),
            pltpu.SemaphoreType.DMA((4,)),
            pltpu.SemaphoreType.DMA((4,)),
            pltpu.SemaphoreType.DMA((4,)),
        ],
        compiler_params=pltpu.CompilerParams(
            collective_id=0, has_side_effects=True, vmem_limit_bytes=52 << 20
        ),
    )(raw_samples, filter_taps, jnp.asarray(table_rows()))
    return visibilities[None]


def solution(mesh):
    return jax.shard_map(
        body,
        mesh=mesh,
        in_specs=(P("inp", "tm"), P()),
        out_specs=P("inp", "tm", None),
        check_vma=False,
    )
```

```python
import math

import jax
import jax.numpy as jnp
import numpy as np
from jax import lax
from jax.experimental import pallas as pl
from jax.experimental.pallas import tpu as pltpu
from jax.sharding import PartitionSpec as P

MESH = pl.DeviceIdType.MESH
NFFT = 2048
TAPS = 4
FRAMES = 32
ALL_FRAMES = 128
PLANE = 64
LANES = 128
TAIL = 8 * (TAPS - 1)
CHUNK = 512
SCALE = 1.0 / math.sqrt(NFFT)


def table_rows():
    row = np.arange(4 * PLANE)
    part, z_hi, dest = row % 2, row // 2 % 2, row // 4
    channel = ((dest // 8) * 2 + z_hi) * 8 + dest % 8
    n = np.arange(NFFT)
    m = (n[None, :] * (channel[:, None] + 1)) % NFFT
    angles = m.astype(np.float32) * np.float32(2.0 * math.pi / NFFT)
    rows = np.where(part[:, None] == 0, np.cos(angles), -np.sin(angles))
    return rows.astype(np.float32).astype(jnp.bfloat16)


def hops(dy, dc, dz=0):
    return min(dy, 8 - dy) + min(dc // 2, 4 - dc // 2) + min(dz, 8 - dz)


def nt(left, right):
    return lax.dot_general(
        left, right, (((1,), (1,)), ((), ())), preferred_element_type=jnp.float32
    )


def nn(left, right):
    return lax.dot_general(
        left, right, (((1,), (0,)), ((), ())), preferred_element_type=jnp.float32
    )


def filter_frames(first, last, taps_v, raw_v, filt_v):
    def step(c, carry):
        base = pl.multiple_of(c * CHUNK, CHUNK)
        taps = [taps_v[k : k + 1, pl.ds(base, CHUNK)] for k in range(TAPS)]

        def frame(f):
            if not 0 <= f < FRAMES:
                return None
            at = pl.multiple_of(base + f * NFFT, CHUNK)
            return raw_v[:, pl.ds(at, CHUNK)].astype(jnp.float32)

        window = [frame(first - k) for k in range(TAPS)]
        done = []
        for f in range(first, last):
            if f > first:
                window = [frame(f)] + window[: TAPS - 1]
            total = jnp.zeros((8, CHUNK), jnp.float32)
            for k in range(TAPS):
                if window[k] is not None:
                    total = total + taps[k] * window[k]
            done.append(total)
            if len(done) == 2:
                pair = jnp.concatenate(done, axis=0).astype(jnp.bfloat16)
                filt_v[(f - 1) * 8 : (f + 1) * 8, pl.ds(base, CHUNK)] = pair
                done = []
        return carry

    lax.fori_loop(0, NFFT // CHUNK, step, 0)


def turn(rows):
    lane = lax.broadcasted_iota(jnp.int32, (8, LANES), 1)
    for b in range(4):
        step, width = 1 << b, 8 << b
        low = (lane & width) == 0
        out = list(rows)
        for s in range(16):
            if s & step == 0:
                x, y = rows[s], rows[s + step]
                out[s] = jnp.where(low, x, pltpu.roll(y, width, 1))
                out[s + step] = jnp.where(low, pltpu.roll(x, LANES - width, 1), y)
        rows = out
    return rows


def kernel(
    raw, taps, table, out,
    raw_v, taps_v, table_v, filt_v, tail_s, tail_r, sbuf, rbuf, xs, xr, lt,
    in_sem, tail_ssem, tail_rsem, ssem, rsem, zssem, zrsem, cssem, fssem, frsem, vouch,
):
    me = lax.axis_index("inp")
    t = lax.axis_index("tm")
    y, zh, xc = me // 16, (me // 8) % 2, me % 8
    mine = y * 8 + xc
    my_m, my_z = mine // 16, zh * 4 + t

    def beside(dc):
        return (xc // 2 + dc // 2) % 4 * 2 + (xc + dc) % 2

    def column(half, at):
        return (y * 16 + half * 8 + xc, at)

    loads = [
        pltpu.make_async_copy(table, table_v, in_sem.at[0]),
        pltpu.make_async_copy(taps, taps_v, in_sem.at[1]),
        pltpu.make_async_copy(raw, raw_v, in_sem.at[2]),
    ]
    for load in loads:
        load.start()

    barrier = pltpu.get_barrier_semaphore()
    offsets = [(0, 0, dz) for dz in range(1, 8)] + [(0, 1, 0)]
    offsets += [(dy, 2 * dx, 0) for dy in range(8) for dx in range(4) if dy + dx]
    for dy, dc, dz in sorted(offsets, key=lambda o: -hops(*o)):
        z = (my_z + dz) % 8
        peer = (((y + dy) % 8) * 16 + (z // 4) * 8 + beside(dc), z % 4)
        pl.semaphore_signal(barrier, inc=1, device_id=peer, device_id_type=MESH)

    for load in loads:
        load.wait()
    filter_frames(FRAMES, FRAMES + 4, taps_v, raw_v, filt_v)
    tail_s[...] = nt(filt_v[8 * FRAMES :, :], table_v[...])[:TAIL]
    filter_frames(0, FRAMES, taps_v, raw_v, filt_v)
    s0 = nt(table_v[...], filt_v[:LANES, :])
    s1 = nt(table_v[...], filt_v[LANES : 2 * LANES, :])

    pl.semaphore_wait(barrier, 39)
    partner = (y * 16 + zh * 8 + beside(1), t)
    pl.semaphore_signal(vouch, inc=1, device_id=partner, device_id_type=MESH)
    tail = pltpu.make_async_remote_copy(
        src_ref=tail_s,
        dst_ref=tail_r,
        send_sem=tail_ssem,
        recv_sem=tail_rsem,
        device_id=(me, (t + 1) % 4),
        device_id_type=MESH,
    )

    @pl.when(t < 3)
    def _():
        tail.start()

    @pl.when(t > 0)
    def _():
        tail.wait_recv()

    @pl.when(t == 0)
    def _():
        tail_r[...] = jnp.zeros_like(tail_r)

    rest = jnp.zeros((LANES - TAIL, 4 * PLANE), jnp.float32)
    s0 = s0 + jnp.concatenate([tail_r[...], rest], axis=0).T
    s0 = (s0 * SCALE).reshape(PLANE // 2, 8, LANES)
    s1 = (s1 * SCALE).reshape(PLANE // 2, 8, LANES)
    first = lax.broadcasted_iota(jnp.int32, (PLANE // 2, 8, LANES), 1) < 4
    sbuf[:, 0] = jnp.where(first, s0, pltpu.roll(s1, 4, 1)).astype(jnp.bfloat16)
    sbuf[:, 1] = jnp.where(first, pltpu.roll(s0, 4, 1), s1).astype(jnp.bfloat16)

    pl.semaphore_wait(vouch, 1)
    own = pltpu.make_async_copy(
        sbuf.at[mine // 2, mine % 2], rbuf.at[mine], rsem.at[my_m]
    )
    own.start()

    order = [(p, dc) for p in range(2) for dc in range(8)]
    order.sort(key=lambda o: -hops(*o))
    for j in range(4):
        for p, dc in order:
            if j + p + dc == 0:
                continue
            to_y = (my_m + j) % 4 * 2 + (y + p) % 2
            to = beside(dc)
            pltpu.make_async_remote_copy(
                src_ref=sbuf.at[to_y * 4 + to // 2, to % 2],
                dst_ref=rbuf.at[mine],
                send_sem=ssem,
                recv_sem=rsem.at[my_m],
                device_id=(to_y * 16 + zh * 8 + to, t),
                device_id_type=MESH,
            ).start()

    sub = lax.broadcasted_iota(jnp.int32, (8, LANES), 0)

    def cross(m):
        for end in (3, 0):
            pltpu.make_async_remote_copy(
                src_ref=xs.at[m, 1 - zh],
                dst_ref=xr.at[m, my_z],
                send_sem=cssem.at[m],
                recv_sem=frsem.at[m * 2 + t // 2],
                device_id=column(1 - zh, end),
                device_id_type=MESH,
            ).start()

    def share(m):
        pltpu.make_async_copy(xs.at[m, zh], xr.at[m, my_z], zrsem.at[m]).start()
        for k in (2, 1, 3):
            pltpu.make_async_remote_copy(
                src_ref=xs.at[m, zh],
                dst_ref=xr.at[m, my_z],
                send_sem=zssem.at[m],
                recv_sem=zrsem.at[m],
                device_id=column(zh, (t + k) % 4),
                device_id_type=MESH,
            ).start()

    def relay(j, carry):
        m = (my_m - j + 4) % 4
        got = rbuf.at[pl.ds(m * 16, 16)]
        pltpu.make_async_copy(got, got, rsem.at[m]).wait()
        rows = turn([rbuf[m * 16 + s].astype(jnp.float32) for s in range(16)])
        halves = ([], [])
        for p in range(8):
            a, b = rows[2 * p], rows[2 * p + 1]
            halves[0].append(jnp.where((sub & 2) == 0, a, pltpu.roll(b, 2, 0)))
            halves[1].append(jnp.where((sub & 2) == 0, pltpu.roll(a, 6, 0), b))
        for h in range(2):
            for q in range(4):
                pair = jnp.concatenate(halves[h][2 * q : 2 * q + 2], axis=0)
                xs[m, h, 16 * q : 16 * q + 16, :] = pair.astype(jnp.bfloat16)

        @pl.when(zh == 0)
        def _():
            share(m)

        @pl.when(zh == 1)
        def _():
            cross(m)

        return carry

    lax.fori_loop(0, 4, relay, 0)

    def drain_cross():
        for m in range(4):
            sent = xr.at[m, pl.ds(0, 2)]
            pltpu.make_async_copy(sent, sent, cssem.at[m]).wait()

    def rest(j, carry):
        m = (my_m - j + 4) % 4

        @pl.when(zh == 0)
        def _():
            cross(m)

        @pl.when(zh == 1)
        def _():
            share(m)

        return carry

    @pl.when(zh == 1)
    def _():
        drain_cross()

    lax.fori_loop(0, 4, rest, 0)

    is_end = jnp.logical_or(t == 0, t == 3)
    nearer = 1 - t // 2

    def pair(m, which):
        return xr.at[m, pl.ds((1 - zh) * 4 + which * 2, 2)]

    def forward(m, inner):
        return pltpu.make_async_remote_copy(
            src_ref=pair(m, nearer),
            dst_ref=pair(m, nearer),
            send_sem=fssem.at[m],
            recv_sem=frsem.at[m * 2 + nearer],
            device_id=column(zh, inner),
            device_id_type=MESH,
        )

    def pass_on(j, carry):
        m = (my_m - j + 4) % 4
        got = pair(m, nearer)
        pltpu.make_async_copy(got, got, frsem.at[m * 2 + nearer]).wait()

        @pl.when(is_end)
        def _():
            forward(m, 2 - t // 3).start()
            forward(m, 1 + t // 3).start()

        return carry

    lax.fori_loop(0, 4, pass_on, 0)

    for m in range(4):
        half = xr.at[m, pl.ds(zh * 4, 4)]
        pltpu.make_async_copy(half, half, zrsem.at[m]).wait()
        got = pair(m, 1 - nearer)
        pltpu.make_async_copy(got, got, frsem.at[m * 2 + 1 - nearer]).wait()

    def block(m):
        both = [xr[m, 4 * z : 4 * z + 4].reshape(256, LANES) for z in range(2)]
        return jnp.concatenate(both, axis=1)

    held = block(t).astype(jnp.float32)
    grouped = held.reshape(32, 8, 256)
    even = lax.broadcasted_iota(jnp.int32, (32, 8, 256), 1) % 2 == 0
    swapped = jnp.where(even, pltpu.roll(grouped, 7, 1), -pltpu.roll(grouped, 1, 1))
    lt[0] = held.T.astype(jnp.bfloat16)
    lt[1] = swapped.reshape(256, 256).T.astype(jnp.bfloat16)

    lane = lax.broadcasted_iota(jnp.int32, (256, LANES), 1)

    def put(m, packed):
        packed = packed * (1.0 / ALL_FRAMES)
        a, b = packed[:, :LANES], packed[:, LANES:]
        base = pl.multiple_of(m * 256, 256)
        tiles = (
            jnp.where(lane < 64, a, pltpu.roll(b, 64, 1)),
            jnp.where(lane < 64, pltpu.roll(a, 64, 1), b),
        )
        for part, tile in enumerate(tiles):
            for z in range(2):
                for half in range(2):
                    out[
                        half * 128 + z * 64 : half * 128 + z * 64 + 64,
                        pl.ds(base + part * LANES, LANES),
                    ] = tile[z * 128 + half * 64 : z * 128 + half * 64 + 64]

    def place(index):
        return (index // 64 % 2) * 128 + (index // 128) * 64 + index % 64

    right = block(t)
    row = place(lax.broadcasted_iota(jnp.int32, (256, 256), 0))
    col = place(lax.broadcasted_iota(jnp.int32, (256, 256), 1))
    put(t, jnp.where(row <= col, nn(lt[0], right), nn(lt[1], right)))

    def other(j, carry):
        m = (t + j) % 4
        put(m, nn(lt[(m < t).astype(jnp.int32)], block(m)))
        return carry

    lax.fori_loop(1, 4, other, 0)

    @pl.when(t < 3)
    def _():
        tail.wait_send()

    sent = rbuf.at[pl.ds(0, PLANE - 1)]
    pltpu.make_async_copy(sent, sent, ssem).wait()
    for m in range(4):
        sent = xr.at[m, pl.ds(0, 3)]
        pltpu.make_async_copy(sent, sent, zssem.at[m]).wait()

    @pl.when(zh == 0)
    def _():
        drain_cross()

    @pl.when(is_end)
    def _():
        for m in range(4):
            sent = xr.at[m, pl.ds(0, 4)]
            pltpu.make_async_copy(sent, sent, fssem.at[m]).wait()


def body(raw_samples, filter_taps):
    anywhere = pl.BlockSpec(memory_space=pl.ANY)
    visibilities = pl.pallas_call(
        kernel,
        out_shape=jax.ShapeDtypeStruct((256, 1024), jnp.float32),
        in_specs=[anywhere] * 3,
        out_specs=pl.BlockSpec(memory_space=pltpu.VMEM),
        scratch_shapes=[
            pltpu.VMEM((8, FRAMES * NFFT), jnp.bfloat16),
            pltpu.VMEM((TAPS, NFFT), jnp.float32),
            pltpu.VMEM((4 * PLANE, NFFT), jnp.bfloat16),
            pltpu.VMEM((8 * FRAMES + 32, NFFT), jnp.bfloat16),
            pltpu.VMEM((TAIL, 4 * PLANE), jnp.float32),
            pltpu.VMEM((TAIL, 4 * PLANE), jnp.float32),
            pltpu.VMEM((PLANE // 2, 2, 8, LANES), jnp.bfloat16),
            pltpu.VMEM((PLANE, 8, LANES), jnp.bfloat16),
            pltpu.VMEM((4, 2, 64, LANES), jnp.bfloat16),
            pltpu.VMEM((4, 8, 64, LANES), jnp.bfloat16),
            pltpu.VMEM((2, 256, 256), jnp.bfloat16),
            pltpu.SemaphoreType.DMA((3,)),
            pltpu.SemaphoreType.DMA,
            pltpu.SemaphoreType.DMA,
            pltpu.SemaphoreType.DMA,
            pltpu.SemaphoreType.DMA((4,)),
            pltpu.SemaphoreType.DMA((4,)),
            pltpu.SemaphoreType.DMA((4,)),
            pltpu.SemaphoreType.DMA((4,)),
            pltpu.SemaphoreType.DMA((4,)),
            pltpu.SemaphoreType.DMA((8,)),
            pltpu.SemaphoreType.REGULAR,
        ],
        compiler_params=pltpu.CompilerParams(
            collective_id=0, has_side_effects=True, vmem_limit_bytes=52 << 20
        ),
    )(raw_samples, pltpu.with_memory_space_constraint(filter_taps, pltpu.HBM), jnp.asarray(table_rows()))
    return visibilities[None]


def solution(mesh):
    return jax.shard_map(
        body,
        mesh=mesh,
        in_specs=(P("inp", "tm"), P()),
        out_specs=P("inp", "tm", None),
        check_vma=False,
    )
```

```python
import math

import jax
import jax.numpy as jnp
import numpy as np
from jax import lax
from jax.experimental import pallas as pl
from jax.experimental.pallas import tpu as pltpu
from jax.sharding import PartitionSpec as P

MESH = pl.DeviceIdType.MESH
NFFT = 2048
TAPS = 4
FRAMES = 32
ALL_FRAMES = 128
PLANE = 64
LANES = 128
TAIL = 8 * (TAPS - 1)
CHUNK = 512
STEPS = (0, 1, 2, 3)
SCALE = 1.0 / math.sqrt(NFFT)


def table_rows():
    row = np.arange(4 * PLANE)
    part, core, dest = row % 2, row // 2 % 2, row // 4
    y, x, z_hi = dest // 8, dest // 2 % 4, dest % 2
    channel = ((y * 2 + z_hi) * 4 + x) * 2 + core
    n = np.arange(NFFT)
    m = (n[None, :] * (channel[:, None] + 1)) % NFFT
    angles = m.astype(np.float32) * np.float32(2.0 * math.pi / NFFT)
    rows = np.where(part[:, None] == 0, np.cos(angles), -np.sin(angles))
    return rows.astype(np.float32).astype(jnp.bfloat16)


def hops(dy, dc, dz=0):
    return min(dy, 8 - dy) + min(dc // 2, 4 - dc // 2) + min(dz, 8 - dz)


def nt(left, right):
    return lax.dot_general(
        left, right, (((1,), (1,)), ((), ())), preferred_element_type=jnp.float32
    )


def nn(left, right):
    return lax.dot_general(
        left, right, (((1,), (0,)), ((), ())), preferred_element_type=jnp.float32
    )


def filter_frames(first, last, taps_v, raw_v, filt_v):
    def step(c, carry):
        base = pl.multiple_of(c * CHUNK, CHUNK)
        taps = [taps_v[k : k + 1, pl.ds(base, CHUNK)] for k in range(TAPS)]

        def frame(f):
            if not 0 <= f < FRAMES:
                return None
            at = pl.multiple_of(base + f * NFFT, CHUNK)
            return raw_v[:, pl.ds(at, CHUNK)].astype(jnp.float32)

        window = [frame(first - k) for k in range(TAPS)]
        done = []
        for f in range(first, last):
            if f > first:
                window = [frame(f)] + window[: TAPS - 1]
            total = jnp.zeros((8, CHUNK), jnp.float32)
            for k in range(TAPS):
                if window[k] is not None:
                    total = total + taps[k] * window[k]
            done.append(total)
            if len(done) == 2:
                pair = jnp.concatenate(done, axis=0).astype(jnp.bfloat16)
                filt_v[(f - 1) * 8 : (f + 1) * 8, pl.ds(base, CHUNK)] = pair
                done = []
        return carry

    lax.fori_loop(0, NFFT // CHUNK, step, 0)


def turn(rows):
    lane = lax.broadcasted_iota(jnp.int32, (8, LANES), 1)
    for b in range(4):
        step, width = 1 << b, 8 << b
        low = (lane & width) == 0
        out = list(rows)
        for s in range(16):
            if s & step == 0:
                x, y = rows[s], rows[s + step]
                out[s] = jnp.where(low, x, pltpu.roll(y, width, 1))
                out[s + step] = jnp.where(low, pltpu.roll(x, LANES - width, 1), y)
        rows = out
    return rows


def kernel(
    raw, taps, table, out,
    raw_v, taps_v, table_v, filt_v, tail_s, tail_r, sbuf, rbuf, xs, xr, lt,
    in_sem, tail_ssem, tail_rsem, ssem, rsem, zssem, zrsem, cssem, fssem, frsem, vouch,
):
    me = lax.axis_index("inp")
    t = lax.axis_index("tm")
    y, zh, xc = me // 16, (me // 8) % 2, me % 8
    mine = y * 8 + xc
    my_m, my_z = mine // 16, zh * 4 + t

    def beside(dc):
        return (xc // 2 + dc // 2) % 4 * 2 + (xc + dc) % 2

    core = xc % 2

    def column(half, at, of=core):
        return (y * 16 + half * 8 + xc - core + of, at)

    loads = [
        pltpu.make_async_copy(table, table_v, in_sem.at[0]),
        pltpu.make_async_copy(taps, taps_v, in_sem.at[1]),
        pltpu.make_async_copy(raw, raw_v, in_sem.at[2]),
    ]
    for load in loads:
        load.start()

    barrier = pltpu.get_barrier_semaphore()
    offsets = [(0, 0, dz) for dz in range(1, 8)] + [(dy, 0, 0) for dy in range(1, 8)]
    offsets += [(0, dc, 0) for dc in range(1, 8)]
    for dy, dc, dz in sorted(offsets, key=lambda o: -hops(*o)):
        z = (my_z + dz) % 8
        peer = (((y + dy) % 8) * 16 + (z // 4) * 8 + beside(dc), z % 4)
        pl.semaphore_signal(barrier, inc=1, device_id=peer, device_id_type=MESH)

    for load in loads:
        load.wait()
    filter_frames(FRAMES, FRAMES + 4, taps_v, raw_v, filt_v)
    tail_s[...] = nt(filt_v[8 * FRAMES :, :], table_v[...])[:TAIL]

    pl.semaphore_wait(barrier, 21)
    partner = (y * 16 + zh * 8 + beside(1), t)
    tail = pltpu.make_async_remote_copy(
        src_ref=tail_s,
        dst_ref=tail_r,
        send_sem=tail_ssem,
        recv_sem=tail_rsem,
        device_id=(me, (t + 1) % 4),
        device_id_type=MESH,
    )

    @pl.when(t < 3)
    def _():
        tail.start()

    for dc in (4, 5, 2, 3, 6, 7, 1):
        peer = (y * 16 + zh * 8 + beside(dc), t)
        pl.semaphore_signal(vouch, inc=1, device_id=peer, device_id_type=MESH)

    filter_frames(0, FRAMES, taps_v, raw_v, filt_v)
    both = nt(table_v[...], filt_v[: 2 * LANES, :])
    s0, s1 = both[:, :LANES], both[:, LANES:]

    @pl.when(t > 0)
    def _():
        tail.wait_recv()

    @pl.when(t == 0)
    def _():
        tail_r[...] = jnp.zeros_like(tail_r)

    rest = jnp.zeros((LANES - TAIL, 4 * PLANE), jnp.float32)
    s0 = s0 + jnp.concatenate([tail_r[...], rest], axis=0).T
    s0 = (s0 * SCALE).reshape(PLANE // 2, 8, LANES)
    s1 = (s1 * SCALE).reshape(PLANE // 2, 8, LANES)
    first = lax.broadcasted_iota(jnp.int32, (PLANE // 2, 8, LANES), 1) < 4
    sbuf[:, 0] = jnp.where(first, s0, pltpu.roll(s1, 4, 1)).astype(jnp.bfloat16)
    sbuf[:, 1] = jnp.where(first, pltpu.roll(s0, 4, 1), s1).astype(jnp.bfloat16)

    pl.semaphore_wait(vouch, 7)
    own = pltpu.make_async_copy(
        sbuf.at[mine // 2, mine % 2], rbuf.at[mine], rsem.at[my_m]
    )
    own.start()

    def send(to_y, to):
        pltpu.make_async_remote_copy(
            src_ref=sbuf.at[to_y * 4 + to // 2, to % 2],
            dst_ref=rbuf.at[mine],
            send_sem=ssem,
            recv_sem=rsem.at[my_m],
            device_id=(to_y * 16 + zh * 8 + to, t),
            device_id_type=MESH,
        ).start()

    order = [(p, dx) for p in range(2) for dx in range(4)]
    order.sort(key=lambda o: -hops(o[0], 2 * o[1]))
    for h in range(2):
        for j in STEPS:
            for p, dx in order:
                if j + p + dx:
                    to_y = (my_m + j) % 4 * 2 + (y + p) % 2
                    send(to_y, (xc // 2 + dx) % 4 * 2 + h)
        if h == 0:
            send(y, beside(1))

    sub = lax.broadcasted_iota(jnp.int32, (8, LANES), 0)

    def copy_block(m, of, to, send_sem, recv_sem):
        pltpu.make_async_remote_copy(
            src_ref=xs.at[m, of],
            dst_ref=xr.at[m, my_z],
            send_sem=send_sem,
            recv_sem=recv_sem,
            device_id=to,
            device_id_type=MESH,
        ).start()

    def cross(m, end):
        for of in range(2):
            to = column(1 - zh, end, of)
            copy_block(m, of, to, cssem.at[m], frsem.at[m * 2 + t // 2])

    def share(m):
        pltpu.make_async_copy(xs.at[m, core], xr.at[m, my_z], zrsem.at[m]).start()
        copy_block(m, 1 - core, partner, zssem.at[m], zrsem.at[m])
        for k in (2, 1, 3):
            for of in range(2):
                to = column(zh, (t + k) % 4, of)
                copy_block(m, of, to, zssem.at[m], zrsem.at[m])

    near = 3 - t // 2 * 3

    def relay(j, carry):
        m = (my_m - j + 4) % 4
        got = rbuf.at[pl.ds(m * 16, 16)]
        pltpu.make_async_copy(got, got, rsem.at[m]).wait()
        rows = turn([rbuf[m * 16 + s].astype(jnp.float32) for s in range(16)])
        halves = ([], [])
        for p in range(8):
            a, b = rows[2 * p], rows[2 * p + 1]
            halves[0].append(jnp.where((sub & 2) == 0, a, pltpu.roll(b, 2, 0)))
            halves[1].append(jnp.where((sub & 2) == 0, pltpu.roll(a, 6, 0), b))
        for h in range(2):
            for q in range(4):
                pair = jnp.concatenate(halves[h][2 * q : 2 * q + 2], axis=0)
                xs[m, h, 16 * q : 16 * q + 16, :] = pair.astype(jnp.bfloat16)

        @pl.when(core == zh)
        def _():
            share(m)

        @pl.when(core != zh)
        def _():
            cross(m, near)
            cross(m, 3 - near)

        return carry

    lax.fori_loop(0, 4, relay, 0)

    is_end = jnp.logical_or(t == 0, t == 3)
    nearer = 1 - t // 2

    def pair(m, which):
        return xr.at[m, pl.ds((1 - zh) * 4 + which * 2, 2)]

    def forward(m, inner):
        return pltpu.make_async_remote_copy(
            src_ref=pair(m, nearer),
            dst_ref=pair(m, nearer),
            send_sem=fssem.at[m],
            recv_sem=frsem.at[m * 2 + nearer],
            device_id=column(zh, inner),
            device_id_type=MESH,
        )

    def pass_on(j, carry):
        m = (my_m - j + 4) % 4
        got = pair(m, nearer)
        pltpu.make_async_copy(got, got, frsem.at[m * 2 + nearer]).wait()

        @pl.when(is_end)
        def _():
            forward(m, 2 - t // 3).start()
            forward(m, 1 + t // 3).start()

        return carry

    lax.fori_loop(0, 4, pass_on, 0)

    for m in range(4):
        half = xr.at[m, pl.ds(zh * 4, 4)]
        pltpu.make_async_copy(half, half, zrsem.at[m]).wait()
        got = pair(m, 1 - nearer)
        pltpu.make_async_copy(got, got, frsem.at[m * 2 + 1 - nearer]).wait()

    def block(m):
        both = [xr[m, 4 * z : 4 * z + 4].reshape(256, LANES) for z in range(2)]
        return jnp.concatenate(both, axis=1)

    held = block(t).astype(jnp.float32)
    grouped = held.reshape(32, 8, 256)
    even = lax.broadcasted_iota(jnp.int32, (32, 8, 256), 1) % 2 == 0
    swapped = jnp.where(even, pltpu.roll(grouped, 7, 1), -pltpu.roll(grouped, 1, 1))
    lt[0] = held.T.astype(jnp.bfloat16)
    lt[1] = swapped.reshape(256, 256).T.astype(jnp.bfloat16)

    lane = lax.broadcasted_iota(jnp.int32, (256, LANES), 1)

    def put(m, packed):
        packed = packed * (1.0 / ALL_FRAMES)
        a, b = packed[:, :LANES], packed[:, LANES:]
        base = pl.multiple_of(m * 256, 256)
        tiles = (
            jnp.where(lane < 64, a, pltpu.roll(b, 64, 1)),
            jnp.where(lane < 64, pltpu.roll(a, 64, 1), b),
        )
        for part, tile in enumerate(tiles):
            for z in range(2):
                for half in range(2):
                    out[
                        half * 128 + z * 64 : half * 128 + z * 64 + 64,
                        pl.ds(base + part * LANES, LANES),
                    ] = tile[z * 128 + half * 64 : z * 128 + half * 64 + 64]

    def place(index):
        return (index // 64 % 2) * 128 + (index // 128) * 64 + index % 64

    right = block(t)
    row = place(lax.broadcasted_iota(jnp.int32, (256, 256), 0))
    col = place(lax.broadcasted_iota(jnp.int32, (256, 256), 1))
    put(t, jnp.where(row <= col, nn(lt[0], right), nn(lt[1], right)))

    def other(j, carry):
        m = (t + j) % 4
        put(m, nn(lt[(m < t).astype(jnp.int32)], block(m)))
        return carry

    for j in range(1, 4):
        other(j, 0)

    @pl.when(t < 3)
    def _():
        tail.wait_send()

    sent = rbuf.at[pl.ds(0, PLANE - 1)]
    pltpu.make_async_copy(sent, sent, ssem).wait()
    @pl.when(core == zh)
    def _():
        for m in range(4):
            sent = xr.at[m, pl.ds(0, 7)]
            pltpu.make_async_copy(sent, sent, zssem.at[m]).wait()

    @pl.when(core != zh)
    def _():
        for m in range(4):
            sent = xr.at[m, pl.ds(0, 4)]
            pltpu.make_async_copy(sent, sent, cssem.at[m]).wait()

    @pl.when(is_end)
    def _():
        for m in range(4):
            sent = xr.at[m, pl.ds(0, 4)]
            pltpu.make_async_copy(sent, sent, fssem.at[m]).wait()


def body(raw_samples, filter_taps):
    anywhere = pl.BlockSpec(memory_space=pl.ANY)
    visibilities = pl.pallas_call(
        kernel,
        out_shape=jax.ShapeDtypeStruct((256, 1024), jnp.float32),
        in_specs=[anywhere] * 3,
        out_specs=pl.BlockSpec(memory_space=pltpu.VMEM),
        scratch_shapes=[
            pltpu.VMEM((8, FRAMES * NFFT), jnp.bfloat16),
            pltpu.VMEM((TAPS, NFFT), jnp.float32),
            pltpu.VMEM((4 * PLANE, NFFT), jnp.bfloat16),
            pltpu.VMEM((8 * FRAMES + 32, NFFT), jnp.bfloat16),
            pltpu.VMEM((TAIL, 4 * PLANE), jnp.float32),
            pltpu.VMEM((TAIL, 4 * PLANE), jnp.float32),
            pltpu.VMEM((PLANE // 2, 2, 8, LANES), jnp.bfloat16),
            pltpu.VMEM((PLANE, 8, LANES), jnp.bfloat16),
            pltpu.VMEM((4, 2, 64, LANES), jnp.bfloat16),
            pltpu.VMEM((4, 8, 64, LANES), jnp.bfloat16),
            pltpu.VMEM((2, 256, 256), jnp.bfloat16),
            pltpu.SemaphoreType.DMA((3,)),
            pltpu.SemaphoreType.DMA,
            pltpu.SemaphoreType.DMA,
            pltpu.SemaphoreType.DMA,
            pltpu.SemaphoreType.DMA((4,)),
            pltpu.SemaphoreType.DMA((4,)),
            pltpu.SemaphoreType.DMA((4,)),
            pltpu.SemaphoreType.DMA((4,)),
            pltpu.SemaphoreType.DMA((4,)),
            pltpu.SemaphoreType.DMA((8,)),
            pltpu.SemaphoreType.REGULAR,
        ],
        compiler_params=pltpu.CompilerParams(
            collective_id=0, has_side_effects=True, vmem_limit_bytes=52 << 20
        ),
    )(raw_samples, pltpu.with_memory_space_constraint(filter_taps, pltpu.HBM), jnp.asarray(table_rows()))
    return visibilities[None]


def solution(mesh):
    return jax.shard_map(
        body,
        mesh=mesh,
        in_specs=(P("inp", "tm"), P()),
        out_specs=P("inp", "tm", None),
        check_vma=False,
    )
```

```python
import math

import jax
import jax.numpy as jnp
import numpy as np
from jax import lax
from jax.experimental import pallas as pl
from jax.experimental.pallas import tpu as pltpu
from jax.sharding import PartitionSpec as P

MESH = pl.DeviceIdType.MESH
NFFT = 2048
TAPS = 4
FRAMES = 32
ALL_FRAMES = 128
PLANE = 64
LANES = 128
TAIL = 8 * (TAPS - 1)
CHUNK = 512
STEPS = (0, 3, 2, 1)
SCALE = 1.0 / math.sqrt(NFFT)


def table_rows():
    row = np.arange(4 * PLANE)
    part, core, dest = row % 2, row // 2 % 2, row // 4
    y, x, z_hi = dest // 8, dest // 2 % 4, dest % 2
    channel = ((y * 2 + z_hi) * 4 + x) * 2 + core
    n = np.arange(NFFT)
    m = (n[None, :] * (channel[:, None] + 1)) % NFFT
    angles = m.astype(np.float32) * np.float32(2.0 * math.pi / NFFT)
    rows = np.where(part[:, None] == 0, np.cos(angles), -np.sin(angles))
    return rows.astype(np.float32).astype(jnp.bfloat16)


def hops(dy, dc, dz=0):
    return min(dy, 8 - dy) + min(dc // 2, 4 - dc // 2) + min(dz, 8 - dz)


def nt(left, right):
    return lax.dot_general(
        left, right, (((1,), (1,)), ((), ())), preferred_element_type=jnp.float32
    )


def nn(left, right):
    return lax.dot_general(
        left, right, (((1,), (0,)), ((), ())), preferred_element_type=jnp.float32
    )


def filter_frames(first, last, taps_v, raw_v, filt_v):
    def step(c, carry):
        base = pl.multiple_of(c * CHUNK, CHUNK)
        taps = [taps_v[k : k + 1, pl.ds(base, CHUNK)] for k in range(TAPS)]

        def frame(f):
            if not 0 <= f < FRAMES:
                return None
            at = pl.multiple_of(base + f * NFFT, CHUNK)
            return raw_v[:, pl.ds(at, CHUNK)].astype(jnp.float32)

        window = [frame(first - k) for k in range(TAPS)]
        done = []
        for f in range(first, last):
            if f > first:
                window = [frame(f)] + window[: TAPS - 1]
            total = jnp.zeros((8, CHUNK), jnp.float32)
            for k in range(TAPS):
                if window[k] is not None:
                    total = total + taps[k] * window[k]
            done.append(total)
            if len(done) == 2:
                pair = jnp.concatenate(done, axis=0).astype(jnp.bfloat16)
                filt_v[(f - 1) * 8 : (f + 1) * 8, pl.ds(base, CHUNK)] = pair
                done = []
        return carry

    lax.fori_loop(0, NFFT // CHUNK, step, 0)


def turn(rows):
    lane = lax.broadcasted_iota(jnp.int32, (8, LANES), 1)
    for b in range(4):
        step, width = 1 << b, 8 << b
        low = (lane & width) == 0
        out = list(rows)
        for s in range(16):
            if s & step == 0:
                x, y = rows[s], rows[s + step]
                out[s] = jnp.where(low, x, pltpu.roll(y, width, 1))
                out[s + step] = jnp.where(low, pltpu.roll(x, LANES - width, 1), y)
        rows = out
    return rows


def kernel(
    raw, taps, table, out,
    raw_v, taps_v, table_v, filt_v, tail_s, tail_r, sbuf, rbuf, xs, xr, lt,
    in_sem, tail_ssem, tail_rsem, ssem, rsem, zssem, zrsem, cssem, fssem, frsem, vouch,
):
    me = lax.axis_index("inp")
    t = lax.axis_index("tm")
    y, zh, xc = me // 16, (me // 8) % 2, me % 8
    mine = y * 8 + xc
    my_m, my_z = mine // 16, zh * 4 + t

    def beside(dc):
        return (xc // 2 + dc // 2) % 4 * 2 + (xc + dc) % 2

    core = xc % 2

    def column(half, at, of=core):
        return (y * 16 + half * 8 + xc - core + of, at)

    loads = [
        pltpu.make_async_copy(table, table_v, in_sem.at[0]),
        pltpu.make_async_copy(taps, taps_v, in_sem.at[1]),
        pltpu.make_async_copy(raw, raw_v, in_sem.at[2]),
    ]
    for load in loads:
        load.start()

    barrier = pltpu.get_barrier_semaphore()
    offsets = [(0, 0, dz) for dz in range(1, 8)] + [(dy, 0, 0) for dy in range(1, 8)]
    offsets += [(0, dc, 0) for dc in range(1, 8)]
    for dy, dc, dz in sorted(offsets, key=lambda o: -hops(*o)):
        z = (my_z + dz) % 8
        peer = (((y + dy) % 8) * 16 + (z // 4) * 8 + beside(dc), z % 4)
        pl.semaphore_signal(barrier, inc=1, device_id=peer, device_id_type=MESH)

    for load in loads:
        load.wait()
    filter_frames(FRAMES, FRAMES + 4, taps_v, raw_v, filt_v)
    tail_s[...] = nt(filt_v[8 * FRAMES :, :], table_v[...])[:TAIL]

    pl.semaphore_wait(barrier, 21)
    partner = (y * 16 + zh * 8 + beside(1), t)
    tail = pltpu.make_async_remote_copy(
        src_ref=tail_s,
        dst_ref=tail_r,
        send_sem=tail_ssem,
        recv_sem=tail_rsem,
        device_id=(me, (t + 1) % 4),
        device_id_type=MESH,
    )

    @pl.when(t < 3)
    def _():
        tail.start()

    for dc in (4, 5, 2, 3, 6, 7, 1):
        peer = (y * 16 + zh * 8 + beside(dc), t)
        pl.semaphore_signal(vouch, inc=1, device_id=peer, device_id_type=MESH)

    filter_frames(0, FRAMES, taps_v, raw_v, filt_v)
    both = nt(table_v[...], filt_v[: 2 * LANES, :])
    s0, s1 = both[:, :LANES], both[:, LANES:]

    @pl.when(t > 0)
    def _():
        tail.wait_recv()

    @pl.when(t == 0)
    def _():
        tail_r[...] = jnp.zeros_like(tail_r)

    rest = jnp.zeros((LANES - TAIL, 4 * PLANE), jnp.float32)
    s0 = s0 + jnp.concatenate([tail_r[...], rest], axis=0).T
    s0 = (s0 * SCALE).reshape(PLANE // 2, 8, LANES)
    s1 = (s1 * SCALE).reshape(PLANE // 2, 8, LANES)
    first = lax.broadcasted_iota(jnp.int32, (PLANE // 2, 8, LANES), 1) < 4
    sbuf[:, 0] = jnp.where(first, s0, pltpu.roll(s1, 4, 1)).astype(jnp.bfloat16)
    sbuf[:, 1] = jnp.where(first, pltpu.roll(s0, 4, 1), s1).astype(jnp.bfloat16)

    pl.semaphore_wait(vouch, 7)
    own = pltpu.make_async_copy(
        sbuf.at[mine // 2, mine % 2], rbuf.at[mine], rsem.at[my_m]
    )
    own.start()

    def send(to_y, to):
        pltpu.make_async_remote_copy(
            src_ref=sbuf.at[to_y * 4 + to // 2, to % 2],
            dst_ref=rbuf.at[mine],
            send_sem=ssem,
            recv_sem=rsem.at[my_m],
            device_id=(to_y * 16 + zh * 8 + to, t),
            device_id_type=MESH,
        ).start()

    order = [(p, dx) for p in range(2) for dx in range(4)]
    order.sort(key=lambda o: -hops(o[0], 2 * o[1]))
    for h in range(2):
        for j in STEPS:
            for p, dx in order:
                if j + p + dx:
                    to_y = (my_m + j) % 4 * 2 + (y + p) % 2
                    send(to_y, (xc // 2 + dx) % 4 * 2 + h)
        if h == 0:
            send(y, beside(1))

    sub = lax.broadcasted_iota(jnp.int32, (8, LANES), 0)

    def copy_block(m, of, to, send_sem, recv_sem):
        pltpu.make_async_remote_copy(
            src_ref=xs.at[m, of],
            dst_ref=xr.at[m, my_z],
            send_sem=send_sem,
            recv_sem=recv_sem,
            device_id=to,
            device_id_type=MESH,
        ).start()

    def cross(m, end):
        for of in range(2):
            to = column(1 - zh, end, of)
            copy_block(m, of, to, cssem.at[m], frsem.at[m * 2 + t // 2])

    def share(m):
        pltpu.make_async_copy(xs.at[m, core], xr.at[m, my_z], zrsem.at[m]).start()
        copy_block(m, 1 - core, partner, zssem.at[m], zrsem.at[m])
        for k in (2, 1, 3):
            for of in range(2):
                to = column(zh, (t + k) % 4, of)
                copy_block(m, of, to, zssem.at[m], zrsem.at[m])

    near = 3 - t // 2 * 3

    def relay(j, carry):
        m = (my_m + j) % 4
        got = rbuf.at[pl.ds(m * 16, 16)]
        pltpu.make_async_copy(got, got, rsem.at[m]).wait()
        at = [m * 16 + (s // 8 + zh) % 2 * 8 + s % 8 for s in range(16)]
        rows = turn([rbuf[s].astype(jnp.float32) for s in at])
        halves = ([], [])
        for p in range(8):
            a, b = rows[2 * p], rows[2 * p + 1]
            halves[0].append(jnp.where((sub & 2) == 0, a, pltpu.roll(b, 2, 0)))
            halves[1].append(jnp.where((sub & 2) == 0, pltpu.roll(a, 6, 0), b))
        for h in range(2):
            for q in range(4):
                pair = jnp.concatenate(halves[h][2 * q : 2 * q + 2], axis=0)
                xs[m, h, 16 * q : 16 * q + 16, :] = pair.astype(jnp.bfloat16)

        @pl.when(core == zh)
        def _():
            share(m)

        @pl.when(core != zh)
        def _():
            cross(m, near)
            cross(m, 3 - near)

        return carry

    lax.fori_loop(0, 4, relay, 0)

    is_end = jnp.logical_or(t == 0, t == 3)
    nearer = 1 - t // 2

    def pair(m, which):
        return xr.at[m, pl.ds((1 - zh) * 4 + which * 2, 2)]

    def forward(m, inner):
        return pltpu.make_async_remote_copy(
            src_ref=pair(m, nearer),
            dst_ref=pair(m, nearer),
            send_sem=fssem.at[m],
            recv_sem=frsem.at[m * 2 + nearer],
            device_id=column(zh, inner),
            device_id_type=MESH,
        )

    def pass_on(j, carry):
        m = (my_m + j) % 4
        got = pair(m, nearer)
        pltpu.make_async_copy(got, got, frsem.at[m * 2 + nearer]).wait()

        @pl.when(is_end)
        def _():
            forward(m, 2 - t // 3).start()
            forward(m, 1 + t // 3).start()

        return carry

    lax.fori_loop(0, 4, pass_on, 0)

    for m in range(4):
        half = xr.at[m, pl.ds(zh * 4, 4)]
        pltpu.make_async_copy(half, half, zrsem.at[m]).wait()
        got = pair(m, 1 - nearer)
        pltpu.make_async_copy(got, got, frsem.at[m * 2 + 1 - nearer]).wait()

    low = lax.broadcasted_iota(jnp.int32, (256, LANES), 1) < 64

    def block(m):
        x, y = [
            xr[m, 4 * z : 4 * z + 4].reshape(256, LANES).astype(jnp.float32)
            for z in range(2)
        ]
        tiles = [jnp.where(low, x, y), pltpu.roll(jnp.where(low, y, x), 64, 1)]
        return jnp.concatenate(tiles, axis=1).astype(jnp.bfloat16)

    held = block(t).astype(jnp.float32)
    grouped = held.reshape(32, 8, 256)
    even = lax.broadcasted_iota(jnp.int32, (32, 8, 256), 1) % 2 == 0
    swapped = jnp.where(even, pltpu.roll(grouped, 7, 1), -pltpu.roll(grouped, 1, 1))
    lt[0] = held.T.astype(jnp.bfloat16)
    lt[1] = swapped.reshape(256, 256).T.astype(jnp.bfloat16)

    def put(m, packed):
        base = pl.multiple_of(m * 256, 256)
        out[:, pl.ds(base, 256)] = packed * (1.0 / ALL_FRAMES)

    right = block(t)
    row = lax.broadcasted_iota(jnp.int32, (256, 256), 0)
    col = lax.broadcasted_iota(jnp.int32, (256, 256), 1)
    put(t, jnp.where(row <= col, nn(lt[0], right), nn(lt[1], right)))

    def other(j, carry):
        m = (t + j) % 4
        put(m, nn(lt[(m < t).astype(jnp.int32)], block(m)))
        return carry

    for j in range(1, 4):
        other(j, 0)

    @pl.when(t < 3)
    def _():
        tail.wait_send()

    sent = rbuf.at[pl.ds(0, PLANE - 1)]
    pltpu.make_async_copy(sent, sent, ssem).wait()
    @pl.when(core == zh)
    def _():
        for m in range(4):
            sent = xr.at[m, pl.ds(0, 7)]
            pltpu.make_async_copy(sent, sent, zssem.at[m]).wait()

    @pl.when(core != zh)
    def _():
        for m in range(4):
            sent = xr.at[m, pl.ds(0, 4)]
            pltpu.make_async_copy(sent, sent, cssem.at[m]).wait()

    @pl.when(is_end)
    def _():
        for m in range(4):
            sent = xr.at[m, pl.ds(0, 4)]
            pltpu.make_async_copy(sent, sent, fssem.at[m]).wait()


def body(raw_samples, filter_taps):
    anywhere = pl.BlockSpec(memory_space=pl.ANY)
    visibilities = pl.pallas_call(
        kernel,
        out_shape=jax.ShapeDtypeStruct((256, 1024), jnp.float32),
        in_specs=[anywhere] * 3,
        out_specs=pl.BlockSpec(memory_space=pltpu.VMEM),
        scratch_shapes=[
            pltpu.VMEM((8, FRAMES * NFFT), jnp.bfloat16),
            pltpu.VMEM((TAPS, NFFT), jnp.float32),
            pltpu.VMEM((4 * PLANE, NFFT), jnp.bfloat16),
            pltpu.VMEM((8 * FRAMES + 32, NFFT), jnp.bfloat16),
            pltpu.VMEM((TAIL, 4 * PLANE), jnp.float32),
            pltpu.VMEM((TAIL, 4 * PLANE), jnp.float32),
            pltpu.VMEM((PLANE // 2, 2, 8, LANES), jnp.bfloat16),
            pltpu.VMEM((PLANE, 8, LANES), jnp.bfloat16),
            pltpu.VMEM((4, 2, 64, LANES), jnp.bfloat16),
            pltpu.VMEM((4, 8, 64, LANES), jnp.bfloat16),
            pltpu.VMEM((2, 256, 256), jnp.bfloat16),
            pltpu.SemaphoreType.DMA((3,)),
            pltpu.SemaphoreType.DMA,
            pltpu.SemaphoreType.DMA,
            pltpu.SemaphoreType.DMA,
            pltpu.SemaphoreType.DMA((4,)),
            pltpu.SemaphoreType.DMA((4,)),
            pltpu.SemaphoreType.DMA((4,)),
            pltpu.SemaphoreType.DMA((4,)),
            pltpu.SemaphoreType.DMA((4,)),
            pltpu.SemaphoreType.DMA((8,)),
            pltpu.SemaphoreType.REGULAR,
        ],
        compiler_params=pltpu.CompilerParams(
            collective_id=0, has_side_effects=True, vmem_limit_bytes=52 << 20
        ),
    )(raw_samples, pltpu.with_memory_space_constraint(filter_taps, pltpu.HBM), jnp.asarray(table_rows()))
    return visibilities[None]


def solution(mesh):
    return jax.shard_map(
        body,
        mesh=mesh,
        in_specs=(P("inp", "tm"), P()),
        out_specs=P("inp", "tm", None),
        check_vma=False,
    )
```

```python
import math

import jax
import jax.numpy as jnp
import numpy as np
from jax import lax
from jax.experimental import pallas as pl
from jax.experimental.pallas import tpu as pltpu
from jax.sharding import PartitionSpec as P

MESH = pl.DeviceIdType.MESH
NFFT = 2048
TAPS = 4
FRAMES = 32
ALL_FRAMES = 128
PLANE = 64
LANES = 128
TAIL = 8 * (TAPS - 1)
CHUNK = 512
STEPS = (0, 3, 2, 1)
SCALE = 1.0 / math.sqrt(NFFT)


def table_rows():
    row = np.arange(4 * PLANE)
    part, core, dest = row % 2, row // 2 % 2, row // 4
    y, x, z_hi = dest // 8, dest // 2 % 4, dest % 2
    channel = ((y * 2 + z_hi) * 4 + x) * 2 + core
    n = np.arange(NFFT)
    m = (n[None, :] * (channel[:, None] + 1)) % NFFT
    angles = m.astype(np.float32) * np.float32(2.0 * math.pi / NFFT)
    rows = np.where(part[:, None] == 0, np.cos(angles), -np.sin(angles))
    return rows.astype(np.float32).astype(jnp.bfloat16)


def hops(dy, dc, dz=0):
    return min(dy, 8 - dy) + min(dc // 2, 4 - dc // 2) + min(dz, 8 - dz)


def nt(left, right):
    return lax.dot_general(
        left, right, (((1,), (1,)), ((), ())), preferred_element_type=jnp.float32
    )


def nn(left, right):
    return lax.dot_general(
        left, right, (((1,), (0,)), ((), ())), preferred_element_type=jnp.float32
    )


def filter_frames(first, last, taps_v, raw_v, filt_v):
    def step(c, carry):
        base = pl.multiple_of(c * CHUNK, CHUNK)
        taps = [taps_v[k : k + 1, pl.ds(base, CHUNK)] for k in range(TAPS)]

        def frame(f):
            if not 0 <= f < FRAMES:
                return None
            at = pl.multiple_of(base + f * NFFT, CHUNK)
            return raw_v[:, pl.ds(at, CHUNK)].astype(jnp.float32)

        window = [frame(first - k) for k in range(TAPS)]
        done = []
        for f in range(first, last):
            if f > first:
                window = [frame(f)] + window[: TAPS - 1]
            total = jnp.zeros((8, CHUNK), jnp.float32)
            for k in range(TAPS):
                if window[k] is not None:
                    total = total + taps[k] * window[k]
            done.append(total)
            if len(done) == 2:
                pair = jnp.concatenate(done, axis=0).astype(jnp.bfloat16)
                filt_v[(f - 1) * 8 : (f + 1) * 8, pl.ds(base, CHUNK)] = pair
                done = []
        return carry

    lax.fori_loop(0, NFFT // CHUNK, step, 0)


def turn(rows):
    lane = lax.broadcasted_iota(jnp.int32, (8, LANES), 1)
    for b in range(4):
        step, width = 1 << b, 8 << b
        low = (lane & width) == 0
        out = list(rows)
        for s in range(16):
            if s & step == 0:
                x, y = rows[s], rows[s + step]
                out[s] = jnp.where(low, x, pltpu.roll(y, width, 1))
                out[s + step] = jnp.where(low, pltpu.roll(x, LANES - width, 1), y)
        rows = out
    return rows


def kernel(
    raw, taps, table, out,
    raw_v, taps_v, table_v, filt_v, tail_s, tail_r, sbuf, rbuf, xs, xr, lt,
    in_sem, tail_ssem, tail_rsem, ssem, rsem, zssem, zrsem, cssem, fssem, frsem, vouch,
):
    me = lax.axis_index("inp")
    t = lax.axis_index("tm")
    y, zh, xc = me // 16, (me // 8) % 2, me % 8
    mine = y * 8 + xc
    my_m, my_z = mine // 16, zh * 4 + t

    def beside(dc):
        return (xc // 2 + dc // 2) % 4 * 2 + (xc + dc) % 2

    core = xc % 2

    def column(half, at, of=core):
        return (y * 16 + half * 8 + xc - core + of, at)

    loads = [
        pltpu.make_async_copy(taps, taps_v, in_sem.at[1]),
        pltpu.make_async_copy(raw, raw_v, in_sem.at[2]),
        pltpu.make_async_copy(table, table_v, in_sem.at[0]),
    ]
    for load in loads:
        load.start()

    barrier = pltpu.get_barrier_semaphore()
    offsets = [(0, 0, dz) for dz in range(1, 8)] + [(dy, 0, 0) for dy in range(1, 8)]
    offsets += [(0, dc, 0) for dc in range(1, 8)]
    for dy, dc, dz in sorted(offsets, key=lambda o: -hops(*o)):
        z = (my_z + dz) % 8
        peer = (((y + dy) % 8) * 16 + (z // 4) * 8 + beside(dc), z % 4)
        pl.semaphore_signal(barrier, inc=1, device_id=peer, device_id_type=MESH)

    loads[0].wait()
    loads[1].wait()
    filter_frames(FRAMES, FRAMES + 4, taps_v, raw_v, filt_v)
    loads[2].wait()
    tail_s[...] = nt(filt_v[8 * FRAMES :, :], table_v[...])[:TAIL]

    pl.semaphore_wait(barrier, 21)
    partner = (y * 16 + zh * 8 + beside(1), t)
    tail = pltpu.make_async_remote_copy(
        src_ref=tail_s,
        dst_ref=tail_r,
        send_sem=tail_ssem,
        recv_sem=tail_rsem,
        device_id=(me, (t + 1) % 4),
        device_id_type=MESH,
    )

    @pl.when(t < 3)
    def _():
        tail.start()

    for dc in (4, 5, 2, 3, 6, 7, 1):
        peer = (y * 16 + zh * 8 + beside(dc), t)
        pl.semaphore_signal(vouch, inc=1, device_id=peer, device_id_type=MESH)

    filter_frames(0, FRAMES, taps_v, raw_v, filt_v)
    both = nt(table_v[...], filt_v[: 2 * LANES, :])
    s0, s1 = both[:, :LANES], both[:, LANES:]
    s1 = (s1 * SCALE).reshape(PLANE // 2, 8, LANES)
    s1_turned = pltpu.roll(s1, 4, 1)

    @pl.when(t > 0)
    def _():
        tail.wait_recv()

    @pl.when(t == 0)
    def _():
        tail_r[...] = jnp.zeros_like(tail_r)

    rest = jnp.zeros((LANES - TAIL, 4 * PLANE), jnp.float32)
    s0 = s0 + jnp.concatenate([tail_r[...], rest], axis=0).T
    s0 = (s0 * SCALE).reshape(PLANE // 2, 8, LANES)
    first = lax.broadcasted_iota(jnp.int32, (PLANE // 2, 8, LANES), 1) < 4
    sbuf[:, 0] = jnp.where(first, s0, s1_turned).astype(jnp.bfloat16)
    sbuf[:, 1] = jnp.where(first, pltpu.roll(s0, 4, 1), s1).astype(jnp.bfloat16)

    pl.semaphore_wait(vouch, 7)
    own = pltpu.make_async_copy(
        sbuf.at[mine // 2, mine % 2], rbuf.at[mine], rsem.at[my_m]
    )
    own.start()

    def send(to_y, to):
        pltpu.make_async_remote_copy(
            src_ref=sbuf.at[to_y * 4 + to // 2, to % 2],
            dst_ref=rbuf.at[mine],
            send_sem=ssem,
            recv_sem=rsem.at[my_m],
            device_id=(to_y * 16 + zh * 8 + to, t),
            device_id_type=MESH,
        ).start()

    order = [(p, dx) for p in range(2) for dx in range(4)]
    order.sort(key=lambda o: -hops(o[0], 2 * o[1]))
    for h in range(2):
        for j in STEPS:
            for p, dx in order:
                if j + p + dx:
                    to_y = (my_m + j) % 4 * 2 + (y + p) % 2
                    send(to_y, (xc // 2 + dx) % 4 * 2 + h)
        if h == 0:
            send(y, beside(1))

    sub = lax.broadcasted_iota(jnp.int32, (8, LANES), 0)

    def copy_block(m, of, to, send_sem, recv_sem):
        pltpu.make_async_remote_copy(
            src_ref=xs.at[m, of],
            dst_ref=xr.at[m, my_z],
            send_sem=send_sem,
            recv_sem=recv_sem,
            device_id=to,
            device_id_type=MESH,
        ).start()

    def cross(m, end):
        for of in range(2):
            to = column(1 - zh, end, of)
            copy_block(m, of, to, cssem.at[m], frsem.at[m * 2 + t // 2])

    def share(m):
        pltpu.make_async_copy(xs.at[m, core], xr.at[m, my_z], zrsem.at[m]).start()
        copy_block(m, 1 - core, partner, zssem.at[m], zrsem.at[m])
        for k in (2, 1, 3):
            for of in range(2):
                to = column(zh, (t + k) % 4, of)
                copy_block(m, of, to, zssem.at[m], zrsem.at[m])

    near = 3 - t // 2 * 3

    def relay(j, carry):
        m = (my_m + j) % 4
        got = rbuf.at[pl.ds(m * 16, 16)]
        pltpu.make_async_copy(got, got, rsem.at[m]).wait()
        at = [m * 16 + (s // 8 + zh) % 2 * 8 + s % 8 for s in range(16)]
        rows = turn([rbuf[s].astype(jnp.float32) for s in at])
        halves = ([], [])
        for p in range(8):
            a, b = rows[2 * p], rows[2 * p + 1]
            halves[0].append(jnp.where((sub & 2) == 0, a, pltpu.roll(b, 2, 0)))
            halves[1].append(jnp.where((sub & 2) == 0, pltpu.roll(a, 6, 0), b))
        for h in range(2):
            for q in range(4):
                pair = jnp.concatenate(halves[h][2 * q : 2 * q + 2], axis=0)
                xs[m, h, 16 * q : 16 * q + 16, :] = pair.astype(jnp.bfloat16)

        @pl.when(core == zh)
        def _():
            share(m)

        @pl.when(core != zh)
        def _():
            cross(m, near)
            cross(m, 3 - near)

        return carry

    lax.fori_loop(0, 4, relay, 0)

    is_end = jnp.logical_or(t == 0, t == 3)
    nearer = 1 - t // 2

    def pair(m, which):
        return xr.at[m, pl.ds((1 - zh) * 4 + which * 2, 2)]

    def forward(m, inner):
        return pltpu.make_async_remote_copy(
            src_ref=pair(m, nearer),
            dst_ref=pair(m, nearer),
            send_sem=fssem.at[m],
            recv_sem=frsem.at[m * 2 + nearer],
            device_id=column(zh, inner),
            device_id_type=MESH,
        )

    def pass_on(j, carry):
        m = (my_m + j) % 4
        got = pair(m, nearer)
        pltpu.make_async_copy(got, got, frsem.at[m * 2 + nearer]).wait()

        @pl.when(is_end)
        def _():
            forward(m, 2 - t // 3).start()
            forward(m, 1 + t // 3).start()

        return carry

    lax.fori_loop(0, 4, pass_on, 0)

    for m in range(4):
        half = xr.at[m, pl.ds(zh * 4, 4)]
        pltpu.make_async_copy(half, half, zrsem.at[m]).wait()
        got = pair(m, 1 - nearer)
        pltpu.make_async_copy(got, got, frsem.at[m * 2 + 1 - nearer]).wait()

    low = lax.broadcasted_iota(jnp.int32, (256, LANES), 1) < 64

    def block(m):
        x, y = [
            xr[m, 4 * z : 4 * z + 4].reshape(256, LANES).astype(jnp.float32)
            for z in range(2)
        ]
        tiles = [jnp.where(low, x, y), pltpu.roll(jnp.where(low, y, x), 64, 1)]
        return jnp.concatenate(tiles, axis=1).astype(jnp.bfloat16)

    held = block(t).astype(jnp.float32)
    grouped = held.reshape(32, 8, 256)
    even = lax.broadcasted_iota(jnp.int32, (32, 8, 256), 1) % 2 == 0
    swapped = jnp.where(even, pltpu.roll(grouped, 7, 1), -pltpu.roll(grouped, 1, 1))
    lt[0] = held.T.astype(jnp.bfloat16)
    lt[1] = swapped.reshape(256, 256).T.astype(jnp.bfloat16)

    def put(m, packed):
        base = pl.multiple_of(m * 256, 256)
        out[:, pl.ds(base, 256)] = packed * (1.0 / ALL_FRAMES)

    right = block(t)
    row = lax.broadcasted_iota(jnp.int32, (256, 256), 0)
    col = lax.broadcasted_iota(jnp.int32, (256, 256), 1)
    put(t, jnp.where(row <= col, nn(lt[0], right), nn(lt[1], right)))

    def other(j, carry):
        m = (t + j) % 4
        put(m, nn(lt[(m < t).astype(jnp.int32)], block(m)))
        return carry

    for j in range(1, 4):
        other(j, 0)

    @pl.when(t < 3)
    def _():
        tail.wait_send()

    sent = rbuf.at[pl.ds(0, PLANE - 1)]
    pltpu.make_async_copy(sent, sent, ssem).wait()
    @pl.when(core == zh)
    def _():
        for m in range(4):
            sent = xr.at[m, pl.ds(0, 7)]
            pltpu.make_async_copy(sent, sent, zssem.at[m]).wait()

    @pl.when(core != zh)
    def _():
        for m in range(4):
            sent = xr.at[m, pl.ds(0, 4)]
            pltpu.make_async_copy(sent, sent, cssem.at[m]).wait()

    @pl.when(is_end)
    def _():
        for m in range(4):
            sent = xr.at[m, pl.ds(0, 4)]
            pltpu.make_async_copy(sent, sent, fssem.at[m]).wait()


def body(raw_samples, filter_taps):
    anywhere = pl.BlockSpec(memory_space=pl.ANY)
    visibilities = pl.pallas_call(
        kernel,
        out_shape=jax.ShapeDtypeStruct((256, 1024), jnp.float32),
        in_specs=[anywhere] * 3,
        out_specs=pl.BlockSpec(memory_space=pltpu.VMEM),
        scratch_shapes=[
            pltpu.VMEM((8, FRAMES * NFFT), jnp.bfloat16),
            pltpu.VMEM((TAPS, NFFT), jnp.float32),
            pltpu.VMEM((4 * PLANE, NFFT), jnp.bfloat16),
            pltpu.VMEM((8 * FRAMES + 32, NFFT), jnp.bfloat16),
            pltpu.VMEM((TAIL, 4 * PLANE), jnp.float32),
            pltpu.VMEM((TAIL, 4 * PLANE), jnp.float32),
            pltpu.VMEM((PLANE // 2, 2, 8, LANES), jnp.bfloat16),
            pltpu.VMEM((PLANE, 8, LANES), jnp.bfloat16),
            pltpu.VMEM((4, 2, 64, LANES), jnp.bfloat16),
            pltpu.VMEM((4, 8, 64, LANES), jnp.bfloat16),
            pltpu.VMEM((2, 256, 256), jnp.bfloat16),
            pltpu.SemaphoreType.DMA((3,)),
            pltpu.SemaphoreType.DMA,
            pltpu.SemaphoreType.DMA,
            pltpu.SemaphoreType.DMA,
            pltpu.SemaphoreType.DMA((4,)),
            pltpu.SemaphoreType.DMA((4,)),
            pltpu.SemaphoreType.DMA((4,)),
            pltpu.SemaphoreType.DMA((4,)),
            pltpu.SemaphoreType.DMA((4,)),
            pltpu.SemaphoreType.DMA((8,)),
            pltpu.SemaphoreType.REGULAR,
        ],
        compiler_params=pltpu.CompilerParams(
            collective_id=0, has_side_effects=True, vmem_limit_bytes=52 << 20
        ),
    )(raw_samples, pltpu.with_memory_space_constraint(filter_taps, pltpu.HBM), jnp.asarray(table_rows()))
    return visibilities[None]


def solution(mesh):
    return jax.shard_map(
        body,
        mesh=mesh,
        in_specs=(P("inp", "tm"), P()),
        out_specs=P("inp", "tm", None),
        check_vma=False,
    )
```
